32 devices in a mesh: seq: 16 (over z, x, core), ch: 2 (over y).
Axes of the slice: x: 2, y: 2, z: 4, core: 2. Of those that a mesh axis runs over, the one named last changes fastest.
Arguments:
- inputs: bfloat16 [256, 8192], P('ch', 'seq'), may hold values from -6 to 6
- proj_weight: bfloat16 [3, 256, 256], P(None, 'ch'), may hold values from -0.5 to 0.5
- short_taps: float32 [256, 3, 3], P('ch'), may hold values from -3 to 3
- skip_gain: float32 [256, 2], P('ch'), may hold values from -1 to 1
- filters: float32 [2, 256, 8192], P(None, 'ch', 'seq'), may hold values from -1 to 1
- out_weight: bfloat16 [256, 256], P('ch'), may hold values from -0.5 to 0.5
Outputs:
- outputs: bfloat16 [256, 8192], P('ch', 'seq')
The draws below stay inside these ranges and needn't reach their ends.
All inputs are finite; a program needn't handle non-finite values.
Results may differ from the reference program's by a relative error of at most 0.007.
Values may be sent and summed in bfloat16 or wider, within the bound.
A program may use at most 64 MiB of HBM per device.

```python
import math
import jax
import jax.numpy as jnp

D = 256
TOKENS = 8192


def draw_filters(key, part):
    base = jax.random.fold_in(key, 7)
    rate_key, noise_key = jax.random.split(base)
    lowest = math.log(1.0 / TOKENS)
    highest = math.log(1.0 / 32.0)
    noise = jnp.clip(jax.random.normal(noise_key, (2, D, TOKENS), jnp.float32), -4.0, 4.0)
    rates = jnp.exp(jax.random.uniform(rate_key, (2, D, 1), jnp.float32, lowest, highest))
    position = jnp.arange(TOKENS, dtype=jnp.float32)[None, None, :]
    return noise * jnp.exp(-rates * position) * jnp.sqrt(1.0 - jnp.exp(-2.0 * rates))


def with_spikes(values, key, source, target, blocks, factor):
    owner, partner = [(jnp.arange(values.shape[dim]) // (values.shape[dim] // blocks)).reshape([-1 if axis == dim else 1 for axis in range(values.ndim)]) for dim in (source, target)]
    chosen = jax.random.permutation(key, blocks)[partner]
    strong = (owner == chosen) | (owner == (partner + blocks // 2) % blocks)
    return jnp.where(strong, factor * values, values)


def block_levels(key, dims, shards, low, high):
    loudness, own = 1.0, jax.random.fold_in(key, 6)
    for axis_at, blocks in shards:
        steps = jnp.exp(jax.random.uniform(jax.random.fold_in(own, axis_at), (blocks,), jnp.float32, low / len(shards), high / len(shards)))
        loudness = loudness * jnp.repeat(steps, dims[axis_at] // blocks).reshape([-1 if axis == axis_at else 1 for axis in range(len(dims))])
    return loudness


def scatter_about(key, shape, scale, reach, cuts=(), kind=jnp.bfloat16):
    drawn = jax.random.normal(key, shape, jnp.float32) * scale
    if len(cuts) > 0:
        drawn = block_levels(key, shape, cuts, -0.22, 0.18) * drawn
    return jnp.clip(drawn, min=-reach, max=reach).astype(kind)


def noise_with(rng, extent, spread, reach, cuts, heavy, held_as=jnp.bfloat16):
    values = spread * jax.random.normal(rng, extent, jnp.float32)
    if cuts:
        values = values * block_levels(rng, extent, cuts, -0.22, 0.18)
    return jnp.clip(with_spikes(values, jax.random.fold_in(rng, 3), *heavy), -reach, reach).astype(held_as)


def setup_inputs(seed: int = 0) -> dict:
    key_of = jax.random.split(jax.random.key(seed), 7)
    return {
        "inputs": scatter_about(key_of[0], (D, TOKENS), 1.0, 6.0, ((0, 2), (1, 16))),
        "proj_weight": noise_with(key_of[1], (3, D, D), D ** -0.5, 0.5, ((1, 2),), (1, 2, 2, 2.0)),
        "short_taps": scatter_about(key_of[2], (D, 3, 3), 0.6, 3.0, ((0, 2),), jnp.float32),
        "skip_gain": jnp.clip(jax.random.uniform(key_of[3], (D, 2), jnp.float32, -1.0, 1.0) * block_levels(key_of[3], (D, 2), ((0, 2),), -0.4, 0.0), -1.0, 1.0),
        "filters": draw_filters(jax.random.fold_in(key_of[6], 71), 0),
        "out_weight": noise_with(key_of[5], (D, D), D ** -0.5, 0.5, ((0, 2),), (0, 1, 2, 2.0)),
    }


def causal_filter(response, signal):
    width = 2 * signal.shape[-1]
    spectrum = jnp.fft.rfft(response, n=width, axis=-1) * jnp.fft.rfft(signal, n=width, axis=-1)
    return jnp.fft.irfft(spectrum, n=width, axis=-1)[:, :signal.shape[-1]].astype(response.dtype)


def reference(inputs, proj_weight, short_taps, skip_gain, filters, out_weight):
    summed = jnp.einsum('sio,it->ost', proj_weight.astype(jnp.float32), inputs.astype(jnp.float32))
    projected = summed.astype(jnp.bfloat16)
    length = inputs.shape[1]
    zeros_head = jnp.zeros((projected.shape[0], 3, 2), jnp.bfloat16)
    padded = jnp.concatenate([zeros_head, projected], axis=2).astype(jnp.float32)
    conv_in = (short_taps[:, :, 0:1] * padded[:, :, 2:] + short_taps[:, :, 1:2] * padded[:, :, 1:-1]
               + short_taps[:, :, 2:3] * padded[:, :, :-2])
    values = conv_in[:, 0, :]
    first_gate = conv_in[:, 1, :]
    second_gate = conv_in[:, 2, :]
    first = causal_filter(filters[0], values) + skip_gain[:, 0:1] * values
    gated = first_gate * first
    second = causal_filter(filters[1], gated) + skip_gain[:, 1:2] * gated
    mixed = (second_gate * second).astype(jnp.bfloat16)
    result = jnp.dot(out_weight.T, mixed, preferred_element_type=jnp.float32)
    return result.astype(jnp.bfloat16)
```

```python
import functools
import math

import jax
import jax.numpy as jnp
from jax import lax
from jax.experimental import pallas as pl
from jax.experimental.pallas import tpu as pltpu
from jax.sharding import PartitionSpec as P

highest = lax.Precision.HIGHEST


def passed_along(shard, axis, by):
    size = lax.axis_size(axis)
    pairs = [(i, i + by) for i in range(size) if 0 <= i + by < size]
    return lax.ppermute(shard, axis, pairs)


def complex_product(left, right):
    return jnp.stack(
        [left[0] * right[0] - left[1] * right[1], left[0] * right[1] + left[1] * right[0]]
    )


def twiddle(spectrum, first_row, total, undo):
    length = spectrum.shape[-1]
    column = jnp.arange(length, dtype=jnp.int32)
    row_index = first_row + jnp.arange(2, dtype=jnp.int32)
    angle = (
        2.0 * math.pi / total * (row_index[:, None] * column[None, :] % total).astype(jnp.float32)
    )
    cosine = jnp.cos(angle)
    sine = jnp.sin(angle)
    real_part = spectrum[0]
    imag_part = spectrum[1]
    if undo:
        return jnp.stack(
            [real_part * cosine - imag_part * sine, real_part * sine + imag_part * cosine]
        )
    return jnp.stack([real_part * cosine + imag_part * sine, imag_part * cosine - real_part * sine])


def local_dft(spectrum, undo):
    length = spectrum.shape[-1]
    width = min(128, length)
    column = jnp.arange(length, dtype=jnp.int32)
    blocks = []
    for block in range(length // width):
        target = block * width + jnp.arange(width, dtype=jnp.int32)
        angle = (
            2.0
            * math.pi
            / length
            * (column[:, None] * target[None, :] % length).astype(jnp.float32)
        )
        table = jnp.stack([jnp.cos(angle), jnp.sin(angle)])
        products = jnp.einsum("xrem,ymd->xyred", spectrum, table, precision=highest)
        if undo:
            blocks.append(
                jnp.stack([products[0, 0] - products[1, 1], products[0, 1] + products[1, 0]])
            )
        else:
            blocks.append(
                jnp.stack([products[0, 0] + products[1, 1], products[1, 0] - products[0, 1]])
            )
    return jnp.concatenate(blocks, axis=-1)


def forward(signal):
    count = lax.axis_size("seq")
    device = lax.axis_index("seq")
    length = signal.shape[-1]
    total = 2 * count * length
    spread = lax.all_to_all(signal[:, None, :], "seq", split_axis=2, concat_axis=1, tiled=True)
    source = jnp.arange(count, dtype=jnp.int32)
    target = jnp.arange(2 * count, dtype=jnp.int32)
    angle = math.pi / count * (target[:, None] * source[None, :] % (2 * count)).astype(jnp.float32)
    table = jnp.stack([jnp.cos(angle), -jnp.sin(angle)])
    summed = jnp.einsum("xka,rab->xrkb", table, spread, precision=highest)
    state = lax.all_to_all(summed, "seq", split_axis=2, concat_axis=3, tiled=True)
    first_row = 2 * device
    return local_dft(twiddle(state, first_row, total, False), False)


def inverse(spectrum):
    count = lax.axis_size("seq")
    device = lax.axis_index("seq")
    length = spectrum.shape[-1]
    total = 2 * count * length
    first_row = 2 * device
    state = twiddle(local_dft(spectrum, True), first_row, total, True)
    spread = lax.all_to_all(state, "seq", split_axis=3, concat_axis=2, tiled=True)
    source = jnp.arange(count, dtype=jnp.int32)
    target = jnp.arange(2 * count, dtype=jnp.int32)
    angle = math.pi / count * (source[:, None] * target[None, :] % (2 * count)).astype(jnp.float32)
    table = jnp.stack([jnp.cos(angle), -jnp.sin(angle)])
    summed = jnp.einsum("xak,xrkb->rab", table, spread, precision=highest)
    result = lax.all_to_all(summed, "seq", split_axis=1, concat_axis=2, tiled=True)[:, 0, :]
    return result * (1.0 / total)


def local(inputs, proj_weight, short_taps, skip_gain, filters, out_weight):
    channels = inputs.shape[0]
    length = inputs.shape[1]
    columns = proj_weight
    summed = lax.psum_scatter(
        jnp.einsum("sio,it->ost", columns, inputs, preferred_element_type=jnp.float32),
        "ch",
        scatter_dimension=0,
        tiled=True,
    )
    projected = summed.astype(jnp.bfloat16)
    before = passed_along(projected[:, :, length - 2 :], "seq", 1)
    padded = jnp.concatenate([before, projected], axis=2).astype(jnp.float32)
    conv_in = (
        short_taps[:, :, 0:1] * padded[:, :, 2:]
        + short_taps[:, :, 1:2] * padded[:, :, 1:-1]
        + short_taps[:, :, 2:3] * padded[:, :, :-2]
    )
    values = conv_in[:, 0, :]
    first_gate = conv_in[:, 1, :]
    second_gate = conv_in[:, 2, :]
    spectra = forward(jnp.concatenate([values, filters[0], filters[1]], axis=0))
    value_spectrum = spectra[:, :channels]
    first_filter = spectra[:, channels : 2 * channels]
    second_filter = spectra[:, 2 * channels :]
    first = inverse(complex_product(value_spectrum, first_filter)) + skip_gain[:, 0:1] * values
    gated = first_gate * first
    second = inverse(complex_product(forward(gated), second_filter)) + skip_gain[:, 1:2] * gated
    mixed = (second_gate * second).astype(jnp.bfloat16)
    columns = out_weight
    result = lax.psum_scatter(
        jnp.einsum("io,it->ot", columns, mixed, preferred_element_type=jnp.float32),
        "ch",
        scatter_dimension=0,
        tiled=True,
    )
    return result.astype(jnp.bfloat16)


MESH = pl.DeviceIdType.MESH
LANES = 128


def kernel(
    S,
    C,
    in_ref,
    pw_ref,
    taps_ref,
    skip_ref,
    f_ref,
    ow_ref,
    out_ref,
    in_buf,
    pw_buf,
    ow_buf,
    send_f,
    recv_f,
    send_p,
    recv_p,
    send_m,
    recv_m,
    hs,
    ps,
    ms,
    xp,
    toep,
    y_send,
    y_recv,
    f_send,
    f_recv,
    p_send,
    p_recv,
    m_send,
    m_recv,
):
    s = lax.axis_index("seq")
    c = lax.axis_index("ch")
    N = S * C
    me = s * C + c
    CL, L = in_ref.shape
    K = CL // S
    nb = L // LANES
    NB = S * nb

    barrier = pltpu.get_barrier_semaphore()

    def greet(i, carry):
        peer = lax.rem(me + i, N)
        pl.semaphore_signal(
            barrier, inc=1, device_id=(peer // C, lax.rem(peer, C)), device_id_type=MESH
        )
        return carry

    lax.fori_loop(1, N, greet, 0)

    def pack(d, carry):
        rows = pl.ds(pl.multiple_of(d * K, K), K)
        parts = []
        for j in range(nb):
            for f in range(2):
                parts.append(f_ref[f, rows, j * LANES : (j + 1) * LANES])
        send_f[d] = jnp.concatenate(parts, axis=0).astype(jnp.bfloat16)
        return carry

    lax.fori_loop(0, S, pack, 0)
    recv_f[s] = send_f[s]
    own = pl.ds(pl.multiple_of(c * CL, CL), CL)
    in_buf[c] = in_ref[...]
    pw_buf[c] = pw_ref[:, :, own]
    ow_buf[c] = ow_ref[:, own]

    pl.semaphore_wait(barrier, N - 1)

    def swap(i, n, to, slot):
        cut = pl.ds(pl.multiple_of(to * CL, CL), CL)
        source, target = [
            (in_ref, in_buf),
            (pw_ref.at[:, :, cut], pw_buf),
            (ow_ref.at[:, cut], ow_buf),
        ][n]
        return pltpu.make_async_remote_copy(
            src_ref=source,
            dst_ref=target.at[slot],
            send_sem=y_send.at[n, i],
            recv_sem=y_recv.at[n, slot],
            device_id=(s, to),
            device_id_type=MESH,
        )

    for i in range(1, C):
        for n in range(3):
            swap(i, n, lax.rem(c + i, C), c).start()

    def filter_copy(i, to, slot):
        return pltpu.make_async_remote_copy(
            src_ref=send_f.at[to],
            dst_ref=recv_f.at[slot],
            send_sem=f_send.at[i],
            recv_sem=f_recv.at[slot],
            device_id=(to, c),
            device_id_type=MESH,
        )

    def start_filter(i, carry):
        filter_copy(i, lax.rem(s + i, S), s).start()
        return carry

    lax.fori_loop(1, S, start_filter, 0)

    def wait_swap(n):
        for i in range(1, C):
            swap(i, n, lax.rem(c + i, C), lax.rem(c + C - i, C)).wait_recv()

    def group_copy(g, i, to, slot):
        return pltpu.make_async_remote_copy(
            src_ref=send_p.at[g, to],
            dst_ref=recv_p.at[g, slot],
            send_sem=p_send.at[g, i],
            recv_sem=p_recv.at[g, slot],
            device_id=(to, c),
            device_id_type=MESH,
        )

    wait_swap(0)
    wait_swap(1)
    signal = in_buf[...].reshape(C * CL, L)
    for g in range(3):
        weight = pw_buf[:, g].reshape(C * CL, CL)
        part = lax.dot_general(
            weight, signal, (((0,), (0,)), ((), ())), preferred_element_type=jnp.float32
        )
        for d in range(S):
            send_p[g, d] = jnp.concatenate(
                [
                    part[d * K : (d + 1) * K, j * LANES : (j + 1) * LANES]
                    for j in range(nb)
                ],
                axis=0,
            ).astype(jnp.bfloat16)
        recv_p[g, s] = send_p[g, s]

        def start_group(i, carry):
            group_copy(g, i, lax.rem(s + i, S), s).start()
            return carry

        lax.fori_loop(1, S, start_group, 0)

    def wait_filter(i, carry):
        filter_copy(i, lax.rem(s + i, S), lax.rem(s + S - i, S)).wait_recv()
        return carry

    lax.fori_loop(1, S, wait_filter, 0)
    hs[...] = recv_f[...].reshape(NB * 2 * K, LANES).astype(jnp.float32)
    xp[...] = jnp.zeros_like(xp)
    lane = lax.broadcasted_iota(jnp.int32, (LANES, LANES), 1)
    below = lax.broadcasted_iota(jnp.int32, (LANES, LANES), 0)
    upper = lane >= below

    def build(q, carry):
        def block(m, previous):
            row = hs[pl.ds(m * (2 * K) + q, 1), :]
            turned = pltpu.roll(
                jnp.broadcast_to(row, (LANES, LANES)), 0, 1, stride=1, stride_axis=0
            )
            toep[q, pl.ds(pl.multiple_of(m * LANES, LANES), LANES), :] = jnp.where(
                upper, turned, previous
            ).astype(jnp.bfloat16)
            return turned

        lax.fori_loop(0, NB, block, jnp.zeros((LANES, LANES), jnp.float32), unroll=4)
        return carry

    lax.fori_loop(0, 2 * K, build, 0)

    for g in range(3):

        def wait_group(i, carry):
            group_copy(g, i, lax.rem(s + i, S), lax.rem(s + S - i, S)).wait_recv()
            return carry

        lax.fori_loop(1, S, wait_group, 0)
        ps[g] = recv_p[g].reshape(NB * K, LANES).astype(jnp.float32)

    column = lax.broadcasted_iota(jnp.int32, (NB, LANES), 1)
    token_block = lax.broadcasted_iota(jnp.int32, (NB, LANES), 0)

    def delayed(x, by):
        turned = pltpu.roll(x, by, 1)
        carried = jnp.where(token_block == 0, 0.0, pltpu.roll(turned, 1, 0))
        return jnp.where(column < by, carried, turned)

    def long_filter(x, q):
        xp[NB : 2 * NB, 0:LANES] = x
        xp[NB + 1 : 2 * NB + 1, LANES : 2 * LANES] = x
        half = NB // 2
        low = jnp.zeros((NB, LANES), jnp.float32)
        high = jnp.zeros((half, LANES), jnp.float32)
        for p in range(NB // 2):
            block = toep[q, 2 * LANES * p : 2 * LANES * (p + 1), :]
            if 2 * p < half:
                rows = xp[NB - 2 * p : 2 * NB - 2 * p, :].astype(jnp.bfloat16)
                low += jnp.dot(rows, block, preferred_element_type=jnp.float32)
            else:
                rows = xp[NB + half - 2 * p : 2 * NB - 2 * p, :].astype(jnp.bfloat16)
                high += jnp.dot(rows, block, preferred_element_type=jnp.float32)
        return jnp.concatenate([low[:half], low[half:] + high], axis=0)

    def channel(k, carry):
        row = s * K + k
        taps = taps_ref[row]
        gains = skip_ref[pl.ds(row, 1), :]
        conv = []
        for g in range(3):
            x = ps[g, pl.ds(k, NB, stride=K), :]
            conv.append(
                taps[g : g + 1, 0:1] * x
                + taps[g : g + 1, 1:2] * delayed(x, 1)
                + taps[g : g + 1, 2:3] * delayed(x, 2)
            )
        first = long_filter(conv[0], k) + gains[:, 0:1] * conv[0]
        gated = conv[1] * first
        second = long_filter(gated, K + k) + gains[:, 1:2] * gated
        ms[pl.ds(k, NB, stride=K), :] = conv[2] * second
        return carry

    lax.fori_loop(0, K, channel, 0)

    def mixed_copy(i, slot):
        peer = lax.rem(me + i, N)
        to = peer // C
        return pltpu.make_async_remote_copy(
            src_ref=send_m.at[to],
            dst_ref=recv_m.at[slot],
            send_sem=m_send.at[i],
            recv_sem=m_recv.at[slot],
            device_id=(to, lax.rem(peer, C)),
            device_id_type=MESH,
        )

    send_m[...] = ms[...].reshape(S, nb * K, LANES).astype(jnp.bfloat16)

    def start_mixed(i, carry):
        mixed_copy(i, c * S + s).start()
        return carry

    lax.fori_loop(1, N, start_mixed, 0)
    recv_m[c * S + s] = send_m[s]
    wait_swap(2)
    weight = ow_buf[...].reshape(C * CL, CL)

    def wait_mixed(i, carry):
        peer = lax.rem(me + N - i, N)
        mixed_copy(i, lax.rem(peer, C) * S + peer // C).wait_recv()
        return carry

    lax.fori_loop(1, N, wait_mixed, 0)
    mixed = recv_m[...].astype(jnp.float32)
    mixed = jnp.concatenate(
        [mixed[:, j * K : (j + 1) * K, :].reshape(N * K, LANES) for j in range(nb)],
        axis=1,
    ).astype(jnp.bfloat16)
    out_ref[...] = lax.dot_general(
        weight, mixed, (((0,), (0,)), ((), ())), preferred_element_type=jnp.float32
    ).astype(out_ref.dtype)

    for i in range(1, C):
        for n in range(3):
            swap(i, n, lax.rem(c + i, C), c).wait_send()

    def drain(i, carry):
        filter_copy(i, lax.rem(s + i, S), s).wait_send()
        for g in range(3):
            group_copy(g, i, lax.rem(s + i, S), s).wait_send()
        return carry

    lax.fori_loop(1, S, drain, 0)

    def drain_mixed(i, carry):
        mixed_copy(i, c * S + s).wait_send()
        return carry

    lax.fori_loop(1, N, drain_mixed, 0)


def fused(S, C, inputs, proj_weight, short_taps, skip_gain, filters, out_weight):
    CL, L = inputs.shape
    K = CL // S
    nb = L // LANES
    NB = S * nb
    N = S * C
    half, full = jnp.bfloat16, jnp.float32
    dma = pltpu.SemaphoreType.DMA
    vmem = pl.BlockSpec(memory_space=pltpu.VMEM)
    return pl.pallas_call(
        functools.partial(kernel, S, C),
        out_shape=jax.ShapeDtypeStruct((CL, L), half),
        in_specs=[vmem] * 6,
        out_specs=vmem,
        scratch_shapes=[
            pltpu.VMEM((C, CL, L), half),
            pltpu.VMEM((C, 3, CL, CL), half),
            pltpu.VMEM((C, CL, CL), half),
            pltpu.VMEM((S, nb * 2 * K, LANES), half),
            pltpu.VMEM((S, nb * 2 * K, LANES), half),
            pltpu.VMEM((3, S, nb * K, LANES), half),
            pltpu.VMEM((3, S, nb * K, LANES), half),
            pltpu.VMEM((S, nb * K, LANES), half),
            pltpu.VMEM((N, nb * K, LANES), half),
            pltpu.VMEM((NB * 2 * K, LANES), full),
            pltpu.VMEM((3, NB * K, LANES), full),
            pltpu.VMEM((NB * K, LANES), full),
            pltpu.VMEM((2 * NB + 8, 2 * LANES), full),
            pltpu.VMEM((2 * K, NB * LANES, LANES), half),
            dma((3, C)),
            dma((3, C)),
            dma((S,)),
            dma((S,)),
            dma((3, S)),
            dma((3, S)),
            dma((N,)),
            dma((N,)),
        ],
        compiler_params=pltpu.CompilerParams(
            collective_id=0, has_side_effects=True, vmem_limit_bytes=VMEM_LIMIT
        ),
    )(inputs, proj_weight, short_taps, skip_gain, filters, out_weight)


VMEM_LIMIT = 56 * 1024 * 1024


def fits(S, C, CL, L):
    K = CL // S
    toeplitz = 2 * K * S * L * LANES * 2
    return (
        C > 1
        and S > 1
        and CL % (8 * S) == 0
        and CL % LANES == 0
        and L % LANES == 0
        and (S * L // LANES) % 16 == 0
        and toeplitz <= 40 * 1024 * 1024
    )


def solution(mesh):
    in_specs = (
        P("ch", "seq"),
        P(None, "ch", None),
        P("ch", None, None),
        P("ch", None),
        P(None, "ch", "seq"),
        P("ch", None),
    )
    out_specs = P("ch", "seq")
    S, C = mesh.shape["seq"], mesh.shape["ch"]

    def body(*shards):
        if fits(S, C, *shards[0].shape):
            return fused(S, C, *shards)
        return local(*shards)

    return jax.shard_map(body, mesh=mesh, in_specs=in_specs, out_specs=out_specs, check_vma=False)
```

```python
import functools
import math

import jax
import jax.numpy as jnp
from jax import lax
from jax.experimental import pallas as pl
from jax.experimental.pallas import tpu as pltpu
from jax.sharding import PartitionSpec as P

highest = lax.Precision.HIGHEST


def passed_along(shard, axis, by):
    size = lax.axis_size(axis)
    pairs = [(i, i + by) for i in range(size) if 0 <= i + by < size]
    return lax.ppermute(shard, axis, pairs)


def complex_product(left, right):
    return jnp.stack(
        [left[0] * right[0] - left[1] * right[1], left[0] * right[1] + left[1] * right[0]]
    )


def twiddle(spectrum, first_row, total, undo):
    length = spectrum.shape[-1]
    column = jnp.arange(length, dtype=jnp.int32)
    row_index = first_row + jnp.arange(2, dtype=jnp.int32)
    angle = (
        2.0 * math.pi / total * (row_index[:, None] * column[None, :] % total).astype(jnp.float32)
    )
    cosine = jnp.cos(angle)
    sine = jnp.sin(angle)
    real_part = spectrum[0]
    imag_part = spectrum[1]
    if undo:
        return jnp.stack(
            [real_part * cosine - imag_part * sine, real_part * sine + imag_part * cosine]
        )
    return jnp.stack([real_part * cosine + imag_part * sine, imag_part * cosine - real_part * sine])


def local_dft(spectrum, undo):
    length = spectrum.shape[-1]
    width = min(128, length)
    column = jnp.arange(length, dtype=jnp.int32)
    blocks = []
    for block in range(length // width):
        target = block * width + jnp.arange(width, dtype=jnp.int32)
        angle = (
            2.0
            * math.pi
            / length
            * (column[:, None] * target[None, :] % length).astype(jnp.float32)
        )
        table = jnp.stack([jnp.cos(angle), jnp.sin(angle)])
        products = jnp.einsum("xrem,ymd->xyred", spectrum, table, precision=highest)
        if undo:
            blocks.append(
                jnp.stack([products[0, 0] - products[1, 1], products[0, 1] + products[1, 0]])
            )
        else:
            blocks.append(
                jnp.stack([products[0, 0] + products[1, 1], products[1, 0] - products[0, 1]])
            )
    return jnp.concatenate(blocks, axis=-1)


def forward(signal):
    count = lax.axis_size("seq")
    device = lax.axis_index("seq")
    length = signal.shape[-1]
    total = 2 * count * length
    spread = lax.all_to_all(signal[:, None, :], "seq", split_axis=2, concat_axis=1, tiled=True)
    source = jnp.arange(count, dtype=jnp.int32)
    target = jnp.arange(2 * count, dtype=jnp.int32)
    angle = math.pi / count * (target[:, None] * source[None, :] % (2 * count)).astype(jnp.float32)
    table = jnp.stack([jnp.cos(angle), -jnp.sin(angle)])
    summed = jnp.einsum("xka,rab->xrkb", table, spread, precision=highest)
    state = lax.all_to_all(summed, "seq", split_axis=2, concat_axis=3, tiled=True)
    first_row = 2 * device
    return local_dft(twiddle(state, first_row, total, False), False)


def inverse(spectrum):
    count = lax.axis_size("seq")
    device = lax.axis_index("seq")
    length = spectrum.shape[-1]
    total = 2 * count * length
    first_row = 2 * device
    state = twiddle(local_dft(spectrum, True), first_row, total, True)
    spread = lax.all_to_all(state, "seq", split_axis=3, concat_axis=2, tiled=True)
    source = jnp.arange(count, dtype=jnp.int32)
    target = jnp.arange(2 * count, dtype=jnp.int32)
    angle = math.pi / count * (source[:, None] * target[None, :] % (2 * count)).astype(jnp.float32)
    table = jnp.stack([jnp.cos(angle), -jnp.sin(angle)])
    summed = jnp.einsum("xak,xrkb->rab", table, spread, precision=highest)
    result = lax.all_to_all(summed, "seq", split_axis=1, concat_axis=2, tiled=True)[:, 0, :]
    return result * (1.0 / total)


def local(inputs, proj_weight, short_taps, skip_gain, filters, out_weight):
    channels = inputs.shape[0]
    length = inputs.shape[1]
    columns = proj_weight
    summed = lax.psum_scatter(
        jnp.einsum("sio,it->ost", columns, inputs, preferred_element_type=jnp.float32),
        "ch",
        scatter_dimension=0,
        tiled=True,
    )
    projected = summed.astype(jnp.bfloat16)
    before = passed_along(projected[:, :, length - 2 :], "seq", 1)
    padded = jnp.concatenate([before, projected], axis=2).astype(jnp.float32)
    conv_in = (
        short_taps[:, :, 0:1] * padded[:, :, 2:]
        + short_taps[:, :, 1:2] * padded[:, :, 1:-1]
        + short_taps[:, :, 2:3] * padded[:, :, :-2]
    )
    values = conv_in[:, 0, :]
    first_gate = conv_in[:, 1, :]
    second_gate = conv_in[:, 2, :]
    spectra = forward(jnp.concatenate([values, filters[0], filters[1]], axis=0))
    value_spectrum = spectra[:, :channels]
    first_filter = spectra[:, channels : 2 * channels]
    second_filter = spectra[:, 2 * channels :]
    first = inverse(complex_product(value_spectrum, first_filter)) + skip_gain[:, 0:1] * values
    gated = first_gate * first
    second = inverse(complex_product(forward(gated), second_filter)) + skip_gain[:, 1:2] * gated
    mixed = (second_gate * second).astype(jnp.bfloat16)
    columns = out_weight
    result = lax.psum_scatter(
        jnp.einsum("io,it->ot", columns, mixed, preferred_element_type=jnp.float32),
        "ch",
        scatter_dimension=0,
        tiled=True,
    )
    return result.astype(jnp.bfloat16)


MESH = pl.DeviceIdType.MESH
LANES = 128


def kernel(
    S,
    C,
    in_ref,
    pw_ref,
    taps_ref,
    skip_ref,
    f_ref,
    ow_ref,
    out_ref,
    in_buf,
    pw_buf,
    ow_buf,
    send_f,
    recv_f,
    send_p,
    recv_p,
    send_m,
    recv_m,
    hs,
    ps,
    ms,
    xp,
    toep,
    y_send,
    y_recv,
    f_send,
    f_recv,
    p_send,
    p_recv,
    m_send,
    m_recv,
):
    s = lax.axis_index("seq")
    c = lax.axis_index("ch")
    N = S * C
    me = s * C + c
    CL, L = in_ref.shape
    K = CL // S
    nb = L // LANES
    NB = S * nb

    barrier = pltpu.get_barrier_semaphore()

    def greet(i, carry):
        peer = lax.rem(me + i, N)
        pl.semaphore_signal(
            barrier, inc=1, device_id=(peer // C, lax.rem(peer, C)), device_id_type=MESH
        )
        return carry

    lax.fori_loop(1, N, greet, 0)

    def pack(d, carry):
        rows = pl.ds(pl.multiple_of(d * K, K), K)
        parts = []
        for j in range(nb):
            for f in range(2):
                parts.append(f_ref[f, rows, j * LANES : (j + 1) * LANES])
        send_f[d] = jnp.concatenate(parts, axis=0).astype(jnp.bfloat16)
        return carry

    lax.fori_loop(0, S, pack, 0)
    recv_f[s] = send_f[s]
    own = pl.ds(pl.multiple_of(c * CL, CL), CL)
    in_buf[c] = in_ref[...]
    pw_buf[c] = pw_ref[:, :, own]
    ow_buf[c] = ow_ref[:, own]

    pl.semaphore_wait(barrier, N - 1)

    def swap(i, n, to, slot):
        cut = pl.ds(pl.multiple_of(to * CL, CL), CL)
        source, target = [
            (in_ref, in_buf),
            (pw_ref.at[:, :, cut], pw_buf),
            (ow_ref.at[:, cut], ow_buf),
        ][n]
        return pltpu.make_async_remote_copy(
            src_ref=source,
            dst_ref=target.at[slot],
            send_sem=y_send.at[n, i],
            recv_sem=y_recv.at[n, slot],
            device_id=(s, to),
            device_id_type=MESH,
        )

    for i in range(1, C):
        for n in range(3):
            swap(i, n, lax.rem(c + i, C), c).start()

    def filter_copy(i, to, slot):
        return pltpu.make_async_remote_copy(
            src_ref=send_f.at[to],
            dst_ref=recv_f.at[slot],
            send_sem=f_send.at[i],
            recv_sem=f_recv.at[slot],
            device_id=(to, c),
            device_id_type=MESH,
        )

    def start_filter(i, carry):
        filter_copy(i, lax.rem(s + i, S), s).start()
        return carry

    lax.fori_loop(1, S, start_filter, 0)

    def wait_swap(n):
        for i in range(1, C):
            swap(i, n, lax.rem(c + i, C), lax.rem(c + C - i, C)).wait_recv()

    def group_copy(g, i, to, slot):
        return pltpu.make_async_remote_copy(
            src_ref=send_p.at[g, to],
            dst_ref=recv_p.at[g, slot],
            send_sem=p_send.at[g, i],
            recv_sem=p_recv.at[g, slot],
            device_id=(to, c),
            device_id_type=MESH,
        )

    wait_swap(0)
    wait_swap(1)
    signal = in_buf[...].reshape(C * CL, L)
    for g in range(3):
        weight = pw_buf[:, g].reshape(C * CL, CL)
        part = lax.dot_general(
            weight, signal, (((0,), (0,)), ((), ())), preferred_element_type=jnp.float32
        )
        for d in range(S):
            send_p[g, d] = jnp.concatenate(
                [
                    part[d * K : (d + 1) * K, j * LANES : (j + 1) * LANES]
                    for j in range(nb)
                ],
                axis=0,
            ).astype(jnp.bfloat16)
        recv_p[g, s] = send_p[g, s]

        def start_group(i, carry):
            group_copy(g, i, lax.rem(s + i, S), s).start()
            return carry

        lax.fori_loop(1, S, start_group, 0)

    def wait_filter(i, carry):
        filter_copy(i, lax.rem(s + i, S), lax.rem(s + S - i, S)).wait_recv()
        return carry

    lax.fori_loop(1, S, wait_filter, 0)
    hs[...] = recv_f[...].reshape(NB * 2 * K, LANES).astype(jnp.float32)
    xp[...] = jnp.zeros_like(xp)
    lane = lax.broadcasted_iota(jnp.int32, (16, LANES), 1)
    below = lax.broadcasted_iota(jnp.int32, (16, LANES), 0)
    half = NB // 2

    def build(q, carry):
        def block(m, previous, side):
            row = hs[pl.ds(m * (2 * K) + q, 1), :]
            turned = pltpu.roll(
                jnp.broadcast_to(row, (16, LANES)), 0, 1, stride=1, stride_axis=0
            )
            base = jnp.where(lane >= below, turned, previous[0]).astype(jnp.bfloat16)
            kept = [turned]
            parts = []
            for g in range(LANES // 16):
                moved = base if g == 0 else pltpu.roll(base, 16 * g, 1)
                if g == 0:
                    parts.append(base)
                else:
                    parts.append(jnp.where(lane >= 16 * g, moved, previous[g]))
                    kept.append(moved)
            place = pl.multiple_of((m - side * half) * LANES, LANES)
            toep[q, pl.ds(place, LANES), side * LANES : (side + 1) * LANES] = (
                jnp.concatenate(parts, axis=0)
            )
            return tuple(kept)

        state = (jnp.zeros((16, LANES), jnp.float32),) + tuple(
            jnp.zeros((16, LANES), jnp.bfloat16) for g in range(1, LANES // 16)
        )
        for side in range(2):
            state = lax.fori_loop(
                side * half,
                (side + 1) * half,
                functools.partial(block, side=side),
                state,
                unroll=4,
            )
        return carry

    lax.fori_loop(0, 2 * K, build, 0)

    for g in range(3):

        def wait_group(i, carry):
            group_copy(g, i, lax.rem(s + i, S), lax.rem(s + S - i, S)).wait_recv()
            return carry

        lax.fori_loop(1, S, wait_group, 0)
        ps[g] = recv_p[g].reshape(NB * K, LANES).astype(jnp.float32)

    column = lax.broadcasted_iota(jnp.int32, (NB, LANES), 1)
    token_block = lax.broadcasted_iota(jnp.int32, (NB, LANES), 0)

    def delayed(x, by):
        turned = pltpu.roll(x, by, 1)
        carried = jnp.where(token_block == 0, 0.0, pltpu.roll(turned, 1, 0))
        return jnp.where(column < by, carried, turned)

    def long_filter(x, q, at):
        xp[at, NB : 2 * NB, 0:LANES] = x
        xp[at, NB + 1 : 2 * NB + 1, LANES : 2 * LANES] = x
        rows = jnp.concatenate(
            [
                xp[at, NB - 2 * p : 2 * NB - 2 * p, :].astype(jnp.bfloat16)
                for p in range(half // 2)
            ],
            axis=1,
        )
        both = jnp.dot(rows, toep[q], preferred_element_type=jnp.float32)
        near, far = both[:, :LANES], both[:half, LANES:]
        return jnp.concatenate([near[:half], near[half:] + far], axis=0)

    def channels(pair, carry):
        ks = [2 * pair, 2 * pair + 1]
        conv, gains = [], []
        for k in ks:
            mine = lanes == s * K + k
            taps = jnp.sum(jnp.where(mine, taps_ref[...], 0.0), axis=2, keepdims=True)
            gains.append(
                jnp.sum(jnp.where(mine[0], skip_ref[...], 0.0), axis=1, keepdims=True)
            )
            parts = []
            for g in range(3):
                x = ps[g, pl.ds(k, NB, stride=K), :]
                parts.append(
                    taps[g, 0:1] * x
                    + taps[g, 1:2] * delayed(x, 1)
                    + taps[g, 2:3] * delayed(x, 2)
                )
            conv.append(parts)
        gated = [
            conv[n][1]
            * (long_filter(conv[n][0], ks[n], 2 * n) + gains[n][0:1] * conv[n][0])
            for n in range(2)
        ]
        for n in range(2):
            second = long_filter(gated[n], K + ks[n], 2 * n + 1)
            second = second + gains[n][1:2] * gated[n]
            ms[pl.ds(ks[n], NB, stride=K), :] = conv[n][2] * second
        return carry

    lanes = lax.broadcasted_iota(jnp.int32, (1, 1, taps_ref.shape[2]), 2)
    lax.fori_loop(0, K // 2, channels, 0)

    def mixed_copy(i, slot):
        peer = lax.rem(me + i, N)
        to = peer // C
        return pltpu.make_async_remote_copy(
            src_ref=send_m.at[to],
            dst_ref=recv_m.at[slot],
            send_sem=m_send.at[i],
            recv_sem=m_recv.at[slot],
            device_id=(to, lax.rem(peer, C)),
            device_id_type=MESH,
        )

    send_m[...] = ms[...].reshape(S, nb * K, LANES).astype(jnp.bfloat16)

    def start_mixed(i, carry):
        mixed_copy(i, c * S + s).start()
        return carry

    lax.fori_loop(1, N, start_mixed, 0)
    recv_m[c * S + s] = send_m[s]
    wait_swap(2)
    weight = ow_buf[...].reshape(C * CL, CL)

    def wait_mixed(i, carry):
        peer = lax.rem(me + N - i, N)
        mixed_copy(i, lax.rem(peer, C) * S + peer // C).wait_recv()
        return carry

    lax.fori_loop(1, N, wait_mixed, 0)
    mixed = recv_m[...].astype(jnp.float32)
    mixed = jnp.concatenate(
        [mixed[:, j * K : (j + 1) * K, :].reshape(N * K, LANES) for j in range(nb)],
        axis=1,
    ).astype(jnp.bfloat16)
    out_ref[...] = lax.dot_general(
        weight, mixed, (((0,), (0,)), ((), ())), preferred_element_type=jnp.float32
    ).astype(out_ref.dtype)

    for i in range(1, C):
        for n in range(3):
            swap(i, n, lax.rem(c + i, C), c).wait_send()

    def drain(i, carry):
        filter_copy(i, lax.rem(s + i, S), s).wait_send()
        for g in range(3):
            group_copy(g, i, lax.rem(s + i, S), s).wait_send()
        return carry

    lax.fori_loop(1, S, drain, 0)

    def drain_mixed(i, carry):
        mixed_copy(i, c * S + s).wait_send()
        return carry

    lax.fori_loop(1, N, drain_mixed, 0)


def fused(S, C, inputs, proj_weight, short_taps, skip_gain, filters, out_weight):
    CL, L = inputs.shape
    K = CL // S
    nb = L // LANES
    NB = S * nb
    N = S * C
    half, full = jnp.bfloat16, jnp.float32
    dma = pltpu.SemaphoreType.DMA
    vmem = pl.BlockSpec(memory_space=pltpu.VMEM)
    return pl.pallas_call(
        functools.partial(kernel, S, C),
        out_shape=jax.ShapeDtypeStruct((CL, L), half),
        in_specs=[vmem] * 6,
        out_specs=vmem,
        scratch_shapes=[
            pltpu.VMEM((C, CL, L), half),
            pltpu.VMEM((C, 3, CL, CL), half),
            pltpu.VMEM((C, CL, CL), half),
            pltpu.VMEM((S, nb * 2 * K, LANES), half),
            pltpu.VMEM((S, nb * 2 * K, LANES), half),
            pltpu.VMEM((3, S, nb * K, LANES), half),
            pltpu.VMEM((3, S, nb * K, LANES), half),
            pltpu.VMEM((S, nb * K, LANES), half),
            pltpu.VMEM((N, nb * K, LANES), half),
            pltpu.VMEM((NB * 2 * K, LANES), full),
            pltpu.VMEM((3, NB * K, LANES), full),
            pltpu.VMEM((NB * K, LANES), full),
            pltpu.VMEM((4, 2 * NB + 8, 2 * LANES), full),
            pltpu.VMEM((2 * K, NB // 2 * LANES, 2 * LANES), half),
            dma((3, C)),
            dma((3, C)),
            dma((S,)),
            dma((S,)),
            dma((3, S)),
            dma((3, S)),
            dma((N,)),
            dma((N,)),
        ],
        compiler_params=pltpu.CompilerParams(
            collective_id=0, has_side_effects=True, vmem_limit_bytes=VMEM_LIMIT
        ),
    )(
        inputs,
        proj_weight,
        short_taps.transpose(1, 2, 0),
        skip_gain.T,
        filters,
        out_weight,
    )


VMEM_LIMIT = 56 * 1024 * 1024


def fits(S, C, CL, L):
    K = CL // S
    toeplitz = 2 * K * S * L * LANES * 2
    return (
        C > 1
        and S > 1
        and CL % (8 * S) == 0
        and CL % LANES == 0
        and L % LANES == 0
        and (S * L // LANES) % 16 == 0
        and toeplitz <= 40 * 1024 * 1024
    )


def solution(mesh):
    in_specs = (
        P("ch", "seq"),
        P(None, "ch", None),
        P("ch", None, None),
        P("ch", None),
        P(None, "ch", "seq"),
        P("ch", None),
    )
    out_specs = P("ch", "seq")
    S, C = mesh.shape["seq"], mesh.shape["ch"]

    def body(*shards):
        if fits(S, C, *shards[0].shape):
            return fused(S, C, *shards)
        return local(*shards)

    return jax.shard_map(body, mesh=mesh, in_specs=in_specs, out_specs=out_specs, check_vma=False)
```

```python
import functools
import math

import jax
import jax.numpy as jnp
from jax import lax
from jax.experimental import pallas as pl
from jax.experimental.pallas import tpu as pltpu
from jax.sharding import PartitionSpec as P

highest = lax.Precision.HIGHEST


def passed_along(shard, axis, by):
    size = lax.axis_size(axis)
    pairs = [(i, i + by) for i in range(size) if 0 <= i + by < size]
    return lax.ppermute(shard, axis, pairs)


def complex_product(left, right):
    return jnp.stack(
        [left[0] * right[0] - left[1] * right[1], left[0] * right[1] + left[1] * right[0]]
    )


def twiddle(spectrum, first_row, total, undo):
    length = spectrum.shape[-1]
    column = jnp.arange(length, dtype=jnp.int32)
    row_index = first_row + jnp.arange(2, dtype=jnp.int32)
    angle = (
        2.0 * math.pi / total * (row_index[:, None] * column[None, :] % total).astype(jnp.float32)
    )
    cosine = jnp.cos(angle)
    sine = jnp.sin(angle)
    real_part = spectrum[0]
    imag_part = spectrum[1]
    if undo:
        return jnp.stack(
            [real_part * cosine - imag_part * sine, real_part * sine + imag_part * cosine]
        )
    return jnp.stack([real_part * cosine + imag_part * sine, imag_part * cosine - real_part * sine])


def local_dft(spectrum, undo):
    length = spectrum.shape[-1]
    width = min(128, length)
    column = jnp.arange(length, dtype=jnp.int32)
    blocks = []
    for block in range(length // width):
        target = block * width + jnp.arange(width, dtype=jnp.int32)
        angle = (
            2.0
            * math.pi
            / length
            * (column[:, None] * target[None, :] % length).astype(jnp.float32)
        )
        table = jnp.stack([jnp.cos(angle), jnp.sin(angle)])
        products = jnp.einsum("xrem,ymd->xyred", spectrum, table, precision=highest)
        if undo:
            blocks.append(
                jnp.stack([products[0, 0] - products[1, 1], products[0, 1] + products[1, 0]])
            )
        else:
            blocks.append(
                jnp.stack([products[0, 0] + products[1, 1], products[1, 0] - products[0, 1]])
            )
    return jnp.concatenate(blocks, axis=-1)


def forward(signal):
    count = lax.axis_size("seq")
    device = lax.axis_index("seq")
    length = signal.shape[-1]
    total = 2 * count * length
    spread = lax.all_to_all(signal[:, None, :], "seq", split_axis=2, concat_axis=1, tiled=True)
    source = jnp.arange(count, dtype=jnp.int32)
    target = jnp.arange(2 * count, dtype=jnp.int32)
    angle = math.pi / count * (target[:, None] * source[None, :] % (2 * count)).astype(jnp.float32)
    table = jnp.stack([jnp.cos(angle), -jnp.sin(angle)])
    summed = jnp.einsum("xka,rab->xrkb", table, spread, precision=highest)
    state = lax.all_to_all(summed, "seq", split_axis=2, concat_axis=3, tiled=True)
    first_row = 2 * device
    return local_dft(twiddle(state, first_row, total, False), False)


def inverse(spectrum):
    count = lax.axis_size("seq")
    device = lax.axis_index("seq")
    length = spectrum.shape[-1]
    total = 2 * count * length
    first_row = 2 * device
    state = twiddle(local_dft(spectrum, True), first_row, total, True)
    spread = lax.all_to_all(state, "seq", split_axis=3, concat_axis=2, tiled=True)
    source = jnp.arange(count, dtype=jnp.int32)
    target = jnp.arange(2 * count, dtype=jnp.int32)
    angle = math.pi / count * (source[:, None] * target[None, :] % (2 * count)).astype(jnp.float32)
    table = jnp.stack([jnp.cos(angle), -jnp.sin(angle)])
    summed = jnp.einsum("xak,xrkb->rab", table, spread, precision=highest)
    result = lax.all_to_all(summed, "seq", split_axis=1, concat_axis=2, tiled=True)[:, 0, :]
    return result * (1.0 / total)


def local(inputs, proj_weight, short_taps, skip_gain, filters, out_weight):
    channels = inputs.shape[0]
    length = inputs.shape[1]
    columns = proj_weight
    summed = lax.psum_scatter(
        jnp.einsum("sio,it->ost", columns, inputs, preferred_element_type=jnp.float32),
        "ch",
        scatter_dimension=0,
        tiled=True,
    )
    projected = summed.astype(jnp.bfloat16)
    before = passed_along(projected[:, :, length - 2 :], "seq", 1)
    padded = jnp.concatenate([before, projected], axis=2).astype(jnp.float32)
    conv_in = (
        short_taps[:, :, 0:1] * padded[:, :, 2:]
        + short_taps[:, :, 1:2] * padded[:, :, 1:-1]
        + short_taps[:, :, 2:3] * padded[:, :, :-2]
    )
    values = conv_in[:, 0, :]
    first_gate = conv_in[:, 1, :]
    second_gate = conv_in[:, 2, :]
    spectra = forward(jnp.concatenate([values, filters[0], filters[1]], axis=0))
    value_spectrum = spectra[:, :channels]
    first_filter = spectra[:, channels : 2 * channels]
    second_filter = spectra[:, 2 * channels :]
    first = inverse(complex_product(value_spectrum, first_filter)) + skip_gain[:, 0:1] * values
    gated = first_gate * first
    second = inverse(complex_product(forward(gated), second_filter)) + skip_gain[:, 1:2] * gated
    mixed = (second_gate * second).astype(jnp.bfloat16)
    columns = out_weight
    result = lax.psum_scatter(
        jnp.einsum("io,it->ot", columns, mixed, preferred_element_type=jnp.float32),
        "ch",
        scatter_dimension=0,
        tiled=True,
    )
    return result.astype(jnp.bfloat16)


MESH = pl.DeviceIdType.MESH
LANES = 128
SEG = 32
PARTS = 8


def kernel(
    S,
    C,
    in_ref,
    pw_ref,
    taps_ref,
    skip_ref,
    f_ref,
    ow_ref,
    out_ref,
    in_buf,
    pw_buf,
    ow_buf,
    send_f,
    recv_f,
    send_p,
    recv_p,
    send_m,
    recv_m,
    hs,
    ps,
    ms,
    xp,
    toep,
    heads,
    tails,
    y_send,
    y_recv,
    f_send,
    f_recv,
    p_send,
    p_recv,
    m_send,
    m_recv,
):
    s = lax.axis_index("seq")
    c = lax.axis_index("ch")
    N = S * C
    me = s * C + c
    CL, L = in_ref.shape
    K = CL // S
    nb = L // LANES
    NB = S * nb

    barrier = pltpu.get_barrier_semaphore()

    def greet(i, carry):
        peer = lax.rem(me + i, N)
        pl.semaphore_signal(
            barrier, inc=1, device_id=(peer // C, lax.rem(peer, C)), device_id_type=MESH
        )
        return carry

    lax.fori_loop(1, N, greet, 0)

    def pack(d, carry):
        rows = pl.ds(pl.multiple_of(d * K, K), K)
        parts = []
        for j in range(nb):
            for f in range(2):
                parts.append(f_ref[f, rows, j * LANES : (j + 1) * LANES])
        send_f[d] = jnp.concatenate(parts, axis=0).astype(jnp.bfloat16)
        return carry

    lax.fori_loop(0, S, pack, 0)
    recv_f[s] = send_f[s]
    own = pl.ds(pl.multiple_of(c * CL, CL), CL)
    in_buf[c] = in_ref[...]
    pw_buf[c] = pw_ref[:, :, own]
    ow_buf[c] = ow_ref[:, own]

    pl.semaphore_wait(barrier, N - 1)

    def swap(i, n, to, slot):
        cut = pl.ds(pl.multiple_of(to * CL, CL), CL)
        source, target = [
            (in_ref, in_buf),
            (pw_ref.at[:, :, cut], pw_buf),
            (ow_ref.at[:, cut], ow_buf),
        ][n]
        return pltpu.make_async_remote_copy(
            src_ref=source,
            dst_ref=target.at[slot],
            send_sem=y_send.at[n, i],
            recv_sem=y_recv.at[n, slot],
            device_id=(s, to),
            device_id_type=MESH,
        )

    for i in range(1, C):
        for n in range(3):
            swap(i, n, lax.rem(c + i, C), c).start()

    def filter_copy(i, to, slot):
        return pltpu.make_async_remote_copy(
            src_ref=send_f.at[to],
            dst_ref=recv_f.at[slot],
            send_sem=f_send.at[i],
            recv_sem=f_recv.at[slot],
            device_id=(to, c),
            device_id_type=MESH,
        )

    def start_filter(i, carry):
        filter_copy(i, lax.rem(s + i, S), s).start()
        return carry

    lax.fori_loop(1, S, start_filter, 0)

    def wait_swap(n):
        for i in range(1, C):
            swap(i, n, lax.rem(c + i, C), lax.rem(c + C - i, C)).wait_recv()

    def group_copy(g, i, to, slot):
        return pltpu.make_async_remote_copy(
            src_ref=send_p.at[g, to],
            dst_ref=recv_p.at[g, slot],
            send_sem=p_send.at[g, i],
            recv_sem=p_recv.at[g, slot],
            device_id=(to, c),
            device_id_type=MESH,
        )

    wait_swap(0)
    wait_swap(1)
    signal = in_buf[...].reshape(C * CL, L)
    for g in range(3):
        weight = pw_buf[:, g].reshape(C * CL, CL)
        part = lax.dot_general(
            weight, signal, (((0,), (0,)), ((), ())), preferred_element_type=jnp.float32
        )
        for d in range(S):
            send_p[g, d] = jnp.concatenate(
                [
                    part[d * K : (d + 1) * K, j * LANES : (j + 1) * LANES]
                    for j in range(nb)
                ],
                axis=0,
            ).astype(jnp.bfloat16)
        recv_p[g, s] = send_p[g, s]

        def start_group(i, carry):
            group_copy(g, i, lax.rem(s + i, S), s).start()
            return carry

        lax.fori_loop(1, S, start_group, 0)

    def wait_filter(i, carry):
        filter_copy(i, lax.rem(s + i, S), lax.rem(s + S - i, S)).wait_recv()
        return carry

    lax.fori_loop(1, S, wait_filter, 0)
    hs[...] = recv_f[...].reshape(NB * 2 * K, LANES).astype(jnp.float32)
    xp[...] = jnp.zeros_like(xp)
    U = NB // PARTS
    V = LANES // SEG
    count = U * V
    lane = lax.broadcasted_iota(jnp.int32, (8, LANES), 1)
    below = lax.broadcasted_iota(jnp.int32, (8, LANES), 0)
    wide_lane = lax.broadcasted_iota(jnp.int32, (U, LANES), 1)

    def build(q, carry):
        h = hs[pl.ds(q, NB, stride=2 * K), :]
        last = jnp.zeros((1, LANES), jnp.float32)
        for w in range(PARTS // V):
            for v in range(V):
                here = None
                for n in range(V):
                    rows = h[U * (V * w + n) : U * (V * w + n + 1)]
                    by = SEG * (n - v) % LANES
                    moved = pltpu.roll(rows, by, 1) if by else rows
                    here = moved if n == 0 else jnp.where(wide_lane >= SEG * n, moved, here)
                heads[w, pl.ds(v, U, stride=V), :] = here
                tails[w, pl.ds(v + 1, U, stride=V), :] = pltpu.roll(here, LANES - SEG, 1)
            tails[w, 0:1, :] = jnp.where(
                wide_lane[0:1] < LANES - SEG, here[U - 1 : U], last
            )
            last = here[U - 1 : U]

        @pl.loop(0, count, unroll=4)
        def _(m):
            place = pl.multiple_of((count - 1 - m) * SEG, SEG)
            for w in range(PARTS // V):
                head = jnp.broadcast_to(heads[w, pl.ds(m, 1), :], (8, LANES))
                tail = jnp.broadcast_to(tails[w, pl.ds(m, 1), :], (8, LANES))
                parts = []
                for g in range(SEG // 8):
                    source = jnp.where(lane % SEG + below < SEG - 8 * g, head, tail)
                    parts.append(pltpu.roll(source, 8 * g, 1, stride=1, stride_axis=0))
                toep[q, pl.ds(place, SEG), w * LANES : (w + 1) * LANES] = (
                    jnp.concatenate(parts, axis=0).astype(jnp.bfloat16)
                )

        return carry

    lax.fori_loop(0, 2 * K, build, 0)

    for g in range(3):

        def wait_group(i, carry):
            group_copy(g, i, lax.rem(s + i, S), lax.rem(s + S - i, S)).wait_recv()
            return carry

        lax.fori_loop(1, S, wait_group, 0)
        ps[g] = recv_p[g].reshape(NB * K, LANES).astype(jnp.float32)

    column = lax.broadcasted_iota(jnp.int32, (NB, LANES), 1)
    token_block = lax.broadcasted_iota(jnp.int32, (NB, LANES), 0)

    def delayed(x, by):
        turned = pltpu.roll(x, by, 1)
        carried = jnp.where(token_block == 0, 0.0, pltpu.roll(turned, 1, 0))
        return jnp.where(column < by, carried, turned)

    def down(x, by):
        if by == 0:
            return x
        return jnp.concatenate(
            [jnp.zeros((by, LANES), jnp.float32), x[: NB - by]], axis=0
        )

    segment = column // SEG

    def long_filter(x, q, at):
        for r in range(V):
            by = LANES - SEG * (r + 1)
            xp[at, r, U : U + NB, :] = delayed(x, by) if by else x
        rows = jnp.concatenate(
            [
                jnp.concatenate(
                    [
                        xp[at, r, t + 1 : t + 1 + NB, :].astype(jnp.bfloat16)
                        for t in range(U)
                    ],
                    axis=1,
                )
                for r in range(V)
            ],
            axis=0,
        )
        both = jnp.dot(rows, toep[q], preferred_element_type=jnp.float32)
        total = None
        for d in range(V):
            part = None
            for n in range(V):
                r = (n + d) % V
                piece = sum(
                    down(
                        both[r * NB : (r + 1) * NB, w * LANES : (w + 1) * LANES],
                        U * (V * w + n),
                    )
                    for w in range(PARTS // V)
                )
                part = piece if n == 0 else jnp.where(segment >= n, piece, part)
            part = pltpu.roll(part, SEG * d, 1) if d else part
            total = part if d == 0 else total + part
        return total

    def channels(pair, carry):
        ks = [2 * pair, 2 * pair + 1]
        conv, gains = [], []
        for k in ks:
            mine = lanes == s * K + k
            taps = jnp.sum(jnp.where(mine, taps_ref[...], 0.0), axis=2, keepdims=True)
            gains.append(
                jnp.sum(jnp.where(mine[0], skip_ref[...], 0.0), axis=1, keepdims=True)
            )
            parts = []
            for g in range(3):
                x = ps[g, pl.ds(k, NB, stride=K), :]
                parts.append(
                    taps[g, 0:1] * x
                    + taps[g, 1:2] * delayed(x, 1)
                    + taps[g, 2:3] * delayed(x, 2)
                )
            conv.append(parts)
        gated = [
            conv[n][1]
            * (long_filter(conv[n][0], ks[n], 2 * n) + gains[n][0:1] * conv[n][0])
            for n in range(2)
        ]
        for n in range(2):
            second = long_filter(gated[n], K + ks[n], 2 * n + 1)
            second = second + gains[n][1:2] * gated[n]
            ms[pl.ds(ks[n], NB, stride=K), :] = conv[n][2] * second
        return carry

    lanes = lax.broadcasted_iota(jnp.int32, (1, 1, taps_ref.shape[2]), 2)
    lax.fori_loop(0, K // 2, channels, 0)

    def mixed_copy(i, slot):
        peer = lax.rem(me + i, N)
        to = peer // C
        return pltpu.make_async_remote_copy(
            src_ref=send_m.at[to],
            dst_ref=recv_m.at[slot],
            send_sem=m_send.at[i],
            recv_sem=m_recv.at[slot],
            device_id=(to, lax.rem(peer, C)),
            device_id_type=MESH,
        )

    send_m[...] = ms[...].reshape(S, nb * K, LANES).astype(jnp.bfloat16)

    def start_mixed(i, carry):
        mixed_copy(i, c * S + s).start()
        return carry

    lax.fori_loop(1, N, start_mixed, 0)
    recv_m[c * S + s] = send_m[s]
    wait_swap(2)
    weight = ow_buf[...].reshape(C * CL, CL)

    def wait_mixed(i, carry):
        peer = lax.rem(me + N - i, N)
        mixed_copy(i, lax.rem(peer, C) * S + peer // C).wait_recv()
        return carry

    lax.fori_loop(1, N, wait_mixed, 0)
    mixed = recv_m[...].astype(jnp.float32)
    mixed = jnp.concatenate(
        [mixed[:, j * K : (j + 1) * K, :].reshape(N * K, LANES) for j in range(nb)],
        axis=1,
    ).astype(jnp.bfloat16)
    out_ref[...] = lax.dot_general(
        weight, mixed, (((0,), (0,)), ((), ())), preferred_element_type=jnp.float32
    ).astype(out_ref.dtype)

    for i in range(1, C):
        for n in range(3):
            swap(i, n, lax.rem(c + i, C), c).wait_send()

    def drain(i, carry):
        filter_copy(i, lax.rem(s + i, S), s).wait_send()
        for g in range(3):
            group_copy(g, i, lax.rem(s + i, S), s).wait_send()
        return carry

    lax.fori_loop(1, S, drain, 0)

    def drain_mixed(i, carry):
        mixed_copy(i, c * S + s).wait_send()
        return carry

    lax.fori_loop(1, N, drain_mixed, 0)


def fused(S, C, inputs, proj_weight, short_taps, skip_gain, filters, out_weight):
    CL, L = inputs.shape
    K = CL // S
    nb = L // LANES
    NB = S * nb
    N = S * C
    half, full = jnp.bfloat16, jnp.float32
    dma = pltpu.SemaphoreType.DMA
    vmem = pl.BlockSpec(memory_space=pltpu.VMEM)
    return pl.pallas_call(
        functools.partial(kernel, S, C),
        out_shape=jax.ShapeDtypeStruct((CL, L), half),
        in_specs=[vmem] * 6,
        out_specs=vmem,
        scratch_shapes=[
            pltpu.VMEM((C, CL, L), half),
            pltpu.VMEM((C, 3, CL, CL), half),
            pltpu.VMEM((C, CL, CL), half),
            pltpu.VMEM((S, nb * 2 * K, LANES), half),
            pltpu.VMEM((S, nb * 2 * K, LANES), half),
            pltpu.VMEM((3, S, nb * K, LANES), half),
            pltpu.VMEM((3, S, nb * K, LANES), half),
            pltpu.VMEM((S, nb * K, LANES), half),
            pltpu.VMEM((N, nb * K, LANES), half),
            pltpu.VMEM((NB * 2 * K, LANES), full),
            pltpu.VMEM((3, NB * K, LANES), full),
            pltpu.VMEM((NB * K, LANES), full),
            pltpu.VMEM((4, LANES // SEG, NB + NB // PARTS, LANES), full),
            pltpu.VMEM((2 * K, NB // PARTS * LANES, PARTS * SEG), half),
            pltpu.VMEM((PARTS * SEG // LANES, NB // PARTS * (LANES // SEG), LANES), full),
            pltpu.VMEM(
                (PARTS * SEG // LANES, (NB // PARTS + 2) * (LANES // SEG), LANES), full
            ),
            dma((3, C)),
            dma((3, C)),
            dma((S,)),
            dma((S,)),
            dma((3, S)),
            dma((3, S)),
            dma((N,)),
            dma((N,)),
        ],
        compiler_params=pltpu.CompilerParams(
            collective_id=0, has_side_effects=True, vmem_limit_bytes=VMEM_LIMIT
        ),
    )(
        inputs,
        proj_weight,
        short_taps.transpose(1, 2, 0),
        skip_gain.T,
        filters,
        out_weight,
    )


VMEM_LIMIT = 56 * 1024 * 1024


def fits(S, C, CL, L):
    K = CL // S
    toeplitz = 2 * K * S * L * SEG * 2
    return (
        C > 1
        and S > 1
        and CL % (8 * S) == 0
        and CL % LANES == 0
        and L % LANES == 0
        and (S * L // LANES) % (8 * PARTS) == 0
        and toeplitz <= 40 * 1024 * 1024
    )


def solution(mesh):
    in_specs = (
        P("ch", "seq"),
        P(None, "ch", None),
        P("ch", None, None),
        P("ch", None),
        P(None, "ch", "seq"),
        P("ch", None),
    )
    out_specs = P("ch", "seq")
    S, C = mesh.shape["seq"], mesh.shape["ch"]

    def body(*shards):
        if fits(S, C, *shards[0].shape):
            return fused(S, C, *shards)
        return local(*shards)

    return jax.shard_map(body, mesh=mesh, in_specs=in_specs, out_specs=out_specs, check_vma=False)
```

```python
import functools
import math

import jax
import jax.numpy as jnp
from jax import lax
from jax.experimental import pallas as pl
from jax.experimental.pallas import tpu as pltpu
from jax.sharding import PartitionSpec as P

highest = lax.Precision.HIGHEST


def passed_along(shard, axis, by):
    size = lax.axis_size(axis)
    pairs = [(i, i + by) for i in range(size) if 0 <= i + by < size]
    return lax.ppermute(shard, axis, pairs)


def complex_product(left, right):
    return jnp.stack(
        [left[0] * right[0] - left[1] * right[1], left[0] * right[1] + left[1] * right[0]]
    )


def twiddle(spectrum, first_row, total, undo):
    length = spectrum.shape[-1]
    column = jnp.arange(length, dtype=jnp.int32)
    row_index = first_row + jnp.arange(2, dtype=jnp.int32)
    angle = (
        2.0 * math.pi / total * (row_index[:, None] * column[None, :] % total).astype(jnp.float32)
    )
    cosine = jnp.cos(angle)
    sine = jnp.sin(angle)
    real_part = spectrum[0]
    imag_part = spectrum[1]
    if undo:
        return jnp.stack(
            [real_part * cosine - imag_part * sine, real_part * sine + imag_part * cosine]
        )
    return jnp.stack([real_part * cosine + imag_part * sine, imag_part * cosine - real_part * sine])


def local_dft(spectrum, undo):
    length = spectrum.shape[-1]
    width = min(128, length)
    column = jnp.arange(length, dtype=jnp.int32)
    blocks = []
    for block in range(length // width):
        target = block * width + jnp.arange(width, dtype=jnp.int32)
        angle = (
            2.0
            * math.pi
            / length
            * (column[:, None] * target[None, :] % length).astype(jnp.float32)
        )
        table = jnp.stack([jnp.cos(angle), jnp.sin(angle)])
        products = jnp.einsum("xrem,ymd->xyred", spectrum, table, precision=highest)
        if undo:
            blocks.append(
                jnp.stack([products[0, 0] - products[1, 1], products[0, 1] + products[1, 0]])
            )
        else:
            blocks.append(
                jnp.stack([products[0, 0] + products[1, 1], products[1, 0] - products[0, 1]])
            )
    return jnp.concatenate(blocks, axis=-1)


def forward(signal):
    count = lax.axis_size("seq")
    device = lax.axis_index("seq")
    length = signal.shape[-1]
    total = 2 * count * length
    spread = lax.all_to_all(signal[:, None, :], "seq", split_axis=2, concat_axis=1, tiled=True)
    source = jnp.arange(count, dtype=jnp.int32)
    target = jnp.arange(2 * count, dtype=jnp.int32)
    angle = math.pi / count * (target[:, None] * source[None, :] % (2 * count)).astype(jnp.float32)
    table = jnp.stack([jnp.cos(angle), -jnp.sin(angle)])
    summed = jnp.einsum("xka,rab->xrkb", table, spread, precision=highest)
    state = lax.all_to_all(summed, "seq", split_axis=2, concat_axis=3, tiled=True)
    first_row = 2 * device
    return local_dft(twiddle(state, first_row, total, False), False)


def inverse(spectrum):
    count = lax.axis_size("seq")
    device = lax.axis_index("seq")
    length = spectrum.shape[-1]
    total = 2 * count * length
    first_row = 2 * device
    state = twiddle(local_dft(spectrum, True), first_row, total, True)
    spread = lax.all_to_all(state, "seq", split_axis=3, concat_axis=2, tiled=True)
    source = jnp.arange(count, dtype=jnp.int32)
    target = jnp.arange(2 * count, dtype=jnp.int32)
    angle = math.pi / count * (source[:, None] * target[None, :] % (2 * count)).astype(jnp.float32)
    table = jnp.stack([jnp.cos(angle), -jnp.sin(angle)])
    summed = jnp.einsum("xak,xrkb->rab", table, spread, precision=highest)
    result = lax.all_to_all(summed, "seq", split_axis=1, concat_axis=2, tiled=True)[:, 0, :]
    return result * (1.0 / total)


def local(inputs, proj_weight, short_taps, skip_gain, filters, out_weight):
    channels = inputs.shape[0]
    length = inputs.shape[1]
    columns = proj_weight
    summed = lax.psum_scatter(
        jnp.einsum("sio,it->ost", columns, inputs, preferred_element_type=jnp.float32),
        "ch",
        scatter_dimension=0,
        tiled=True,
    )
    projected = summed.astype(jnp.bfloat16)
    before = passed_along(projected[:, :, length - 2 :], "seq", 1)
    padded = jnp.concatenate([before, projected], axis=2).astype(jnp.float32)
    conv_in = (
        short_taps[:, :, 0:1] * padded[:, :, 2:]
        + short_taps[:, :, 1:2] * padded[:, :, 1:-1]
        + short_taps[:, :, 2:3] * padded[:, :, :-2]
    )
    values = conv_in[:, 0, :]
    first_gate = conv_in[:, 1, :]
    second_gate = conv_in[:, 2, :]
    spectra = forward(jnp.concatenate([values, filters[0], filters[1]], axis=0))
    value_spectrum = spectra[:, :channels]
    first_filter = spectra[:, channels : 2 * channels]
    second_filter = spectra[:, 2 * channels :]
    first = inverse(complex_product(value_spectrum, first_filter)) + skip_gain[:, 0:1] * values
    gated = first_gate * first
    second = inverse(complex_product(forward(gated), second_filter)) + skip_gain[:, 1:2] * gated
    mixed = (second_gate * second).astype(jnp.bfloat16)
    columns = out_weight
    result = lax.psum_scatter(
        jnp.einsum("io,it->ot", columns, mixed, preferred_element_type=jnp.float32),
        "ch",
        scatter_dimension=0,
        tiled=True,
    )
    return result.astype(jnp.bfloat16)


MESH = pl.DeviceIdType.MESH
LANES = 128
SEG = 32
PARTS = 8


def kernel(
    S,
    C,
    in_ref,
    pw_ref,
    taps_ref,
    skip_ref,
    f_ref,
    ow_ref,
    out_ref,
    in_buf,
    pw_buf,
    ow_buf,
    send_f,
    recv_f,
    send_p,
    recv_p,
    send_m,
    recv_m,
    hs,
    ps,
    ms,
    xp,
    toep,
    heads,
    tails,
    y_send,
    y_recv,
    f_send,
    f_recv,
    p_send,
    p_recv,
    m_send,
    m_recv,
):
    s = lax.axis_index("seq")
    c = lax.axis_index("ch")
    N = S * C
    me = s * C + c
    CL, L = in_ref.shape
    K = CL // S
    nb = L // LANES
    NB = S * nb

    barrier = pltpu.get_barrier_semaphore()

    def greet(i, carry):
        peer = lax.rem(me + i, N)
        pl.semaphore_signal(
            barrier, inc=1, device_id=(peer // C, lax.rem(peer, C)), device_id_type=MESH
        )
        return carry

    lax.fori_loop(1, N, greet, 0)

    def pack(d, carry):
        rows = pl.ds(pl.multiple_of(d * K, K), K)
        parts = []
        for j in range(nb):
            for f in range(2):
                parts.append(f_ref[f, rows, j * LANES : (j + 1) * LANES])
        send_f[d] = jnp.concatenate(parts, axis=0).astype(jnp.bfloat16)
        return carry

    lax.fori_loop(0, S, pack, 0)
    recv_f[s] = send_f[s]
    own = pl.ds(pl.multiple_of(c * CL, CL), CL)
    in_buf[c] = in_ref[...]
    pw_buf[c] = pw_ref[:, :, own]
    ow_buf[c] = ow_ref[:, own]

    pl.semaphore_wait(barrier, N - 1)

    def swap(i, n, to, slot):
        cut = pl.ds(pl.multiple_of(to * CL, CL), CL)
        source, target = [
            (in_ref, in_buf.at[slot]),
            (pw_ref.at[0, :, cut], pw_buf.at[slot, 0]),
            (pw_ref.at[1, :, cut], pw_buf.at[slot, 1]),
            (pw_ref.at[2, :, cut], pw_buf.at[slot, 2]),
            (ow_ref.at[:, cut], ow_buf.at[slot]),
        ][n]
        return pltpu.make_async_remote_copy(
            src_ref=source,
            dst_ref=target,
            send_sem=y_send.at[n, i],
            recv_sem=y_recv.at[n, slot],
            device_id=(s, to),
            device_id_type=MESH,
        )

    for i in range(1, C):
        for n in range(5):
            swap(i, n, lax.rem(c + i, C), c).start()

    def filter_copy(i, to, slot):
        return pltpu.make_async_remote_copy(
            src_ref=send_f.at[to],
            dst_ref=recv_f.at[slot],
            send_sem=f_send.at[i],
            recv_sem=f_recv.at[slot],
            device_id=(to, c),
            device_id_type=MESH,
        )

    def start_filter(i, carry):
        filter_copy(i, lax.rem(s + i, S), s).start()
        return carry

    lax.fori_loop(1, S, start_filter, 0)

    def wait_swap(n):
        for i in range(1, C):
            swap(i, n, lax.rem(c + i, C), lax.rem(c + C - i, C)).wait_recv()

    def group_copy(g, i, to, slot):
        return pltpu.make_async_remote_copy(
            src_ref=send_p.at[g, to],
            dst_ref=recv_p.at[g, slot],
            send_sem=p_send.at[g, i],
            recv_sem=p_recv.at[g, slot],
            device_id=(to, c),
            device_id_type=MESH,
        )

    wait_swap(0)
    signal = in_buf[...].reshape(C * CL, L)
    for g in range(3):
        wait_swap(1 + g)
        weight = pw_buf[:, g].reshape(C * CL, CL)
        part = lax.dot_general(
            weight, signal, (((0,), (0,)), ((), ())), preferred_element_type=jnp.float32
        )
        for d in range(S):
            send_p[g, d] = jnp.concatenate(
                [
                    part[d * K : (d + 1) * K, j * LANES : (j + 1) * LANES]
                    for j in range(nb)
                ],
                axis=0,
            ).astype(jnp.bfloat16)
        recv_p[g, s] = send_p[g, s]

        def start_group(i, carry):
            group_copy(g, i, lax.rem(s + i, S), s).start()
            return carry

        lax.fori_loop(1, S, start_group, 0)

    def wait_filter(i, carry):
        filter_copy(i, lax.rem(s + i, S), lax.rem(s + S - i, S)).wait_recv()
        return carry

    lax.fori_loop(1, S, wait_filter, 0)
    hs[...] = recv_f[...].reshape(NB * 2 * K, LANES).astype(jnp.float32)
    xp[...] = jnp.zeros_like(xp)
    U = NB // PARTS
    V = LANES // SEG
    count = U * V
    lane = lax.broadcasted_iota(jnp.int32, (8, LANES), 1)
    below = lax.broadcasted_iota(jnp.int32, (8, LANES), 0)
    wide_lane = lax.broadcasted_iota(jnp.int32, (U, LANES), 1)

    def build(q, carry):
        h = hs[pl.ds(q, NB, stride=2 * K), :]
        last = jnp.zeros((1, LANES), jnp.float32)
        for w in range(PARTS // V):
            for v in range(V):
                here = None
                for n in range(V):
                    rows = h[U * (V * w + n) : U * (V * w + n + 1)]
                    by = SEG * (n - v) % LANES
                    moved = pltpu.roll(rows, by, 1) if by else rows
                    here = moved if n == 0 else jnp.where(wide_lane >= SEG * n, moved, here)
                heads[w, pl.ds(v, U, stride=V), :] = here
                tails[w, pl.ds(v + 1, U, stride=V), :] = pltpu.roll(here, LANES - SEG, 1)
            tails[w, 0:1, :] = jnp.where(
                wide_lane[0:1] < LANES - SEG, here[U - 1 : U], last
            )
            last = here[U - 1 : U]

        @pl.loop(0, count, unroll=4)
        def _(m):
            place = pl.multiple_of((count - 1 - m) * SEG, SEG)
            for w in range(PARTS // V):
                head = jnp.broadcast_to(heads[w, pl.ds(m, 1), :], (8, LANES))
                tail = jnp.broadcast_to(tails[w, pl.ds(m, 1), :], (8, LANES))
                parts = []
                for g in range(SEG // 8):
                    source = jnp.where(lane % SEG + below < SEG - 8 * g, head, tail)
                    parts.append(pltpu.roll(source, 8 * g, 1, stride=1, stride_axis=0))
                toep[q, pl.ds(place, SEG), w * LANES : (w + 1) * LANES] = (
                    jnp.concatenate(parts, axis=0).astype(jnp.bfloat16)
                )

        return carry

    lax.fori_loop(0, 2 * K, build, 0)

    for g in range(3):

        def wait_group(i, carry):
            group_copy(g, i, lax.rem(s + i, S), lax.rem(s + S - i, S)).wait_recv()
            return carry

        lax.fori_loop(1, S, wait_group, 0)
        ps[g] = recv_p[g].reshape(NB * K, LANES).astype(jnp.float32)

    column = lax.broadcasted_iota(jnp.int32, (NB, LANES), 1)
    token_block = lax.broadcasted_iota(jnp.int32, (NB, LANES), 0)

    def delayed(x, by):
        turned = pltpu.roll(x, by, 1)
        carried = jnp.where(token_block == 0, 0.0, pltpu.roll(turned, 1, 0))
        return jnp.where(column < by, carried, turned)

    def down(x, by):
        if by == 0:
            return x
        return jnp.concatenate(
            [jnp.zeros((by, LANES), jnp.float32), x[: NB - by]], axis=0
        )

    segment = column // SEG

    def long_filter(x, q, at):
        for r in range(V):
            by = LANES - SEG * (r + 1)
            xp[at, r, U : U + NB, :] = delayed(x, by) if by else x
        rows = jnp.concatenate(
            [
                jnp.concatenate(
                    [
                        xp[at, r, t + 1 : t + 1 + NB, :].astype(jnp.bfloat16)
                        for t in range(U)
                    ],
                    axis=1,
                )
                for r in range(V)
            ],
            axis=0,
        )
        both = jnp.dot(rows, toep[q], preferred_element_type=jnp.float32)
        total = None
        for d in range(V):
            part = None
            for n in range(V):
                r = (n + d) % V
                piece = sum(
                    down(
                        both[r * NB : (r + 1) * NB, w * LANES : (w + 1) * LANES],
                        U * (V * w + n),
                    )
                    for w in range(PARTS // V)
                )
                part = piece if n == 0 else jnp.where(segment >= n, piece, part)
            part = pltpu.roll(part, SEG * d, 1) if d else part
            total = part if d == 0 else total + part
        return total

    def channels(pair, carry):
        ks = [2 * pair, 2 * pair + 1]
        conv, gains = [], []
        for k in ks:
            mine = lanes == s * K + k
            taps = jnp.sum(jnp.where(mine, taps_ref[...], 0.0), axis=2, keepdims=True)
            gains.append(
                jnp.sum(jnp.where(mine[0], skip_ref[...], 0.0), axis=1, keepdims=True)
            )
            parts = []
            for g in range(3):
                x = ps[g, pl.ds(k, NB, stride=K), :]
                parts.append(
                    taps[g, 0:1] * x
                    + taps[g, 1:2] * delayed(x, 1)
                    + taps[g, 2:3] * delayed(x, 2)
                )
            conv.append(parts)
        gated = [
            conv[n][1]
            * (long_filter(conv[n][0], ks[n], 2 * n) + gains[n][0:1] * conv[n][0])
            for n in range(2)
        ]
        for n in range(2):
            second = long_filter(gated[n], K + ks[n], 2 * n + 1)
            second = second + gains[n][1:2] * gated[n]
            ms[pl.ds(ks[n], NB, stride=K), :] = conv[n][2] * second
        return carry

    lanes = lax.broadcasted_iota(jnp.int32, (1, 1, taps_ref.shape[2]), 2)
    lax.fori_loop(0, K // 2, channels, 0)

    def mixed_copy(i, slot):
        peer = lax.rem(me + i, N)
        to = peer // C
        return pltpu.make_async_remote_copy(
            src_ref=send_m.at[to],
            dst_ref=recv_m.at[slot],
            send_sem=m_send.at[i],
            recv_sem=m_recv.at[slot],
            device_id=(to, lax.rem(peer, C)),
            device_id_type=MESH,
        )

    send_m[...] = ms[...].reshape(S, nb * K, LANES).astype(jnp.bfloat16)

    def start_mixed(i, carry):
        mixed_copy(i, c * S + s).start()
        return carry

    lax.fori_loop(1, N, start_mixed, 0)
    recv_m[c * S + s] = send_m[s]
    wait_swap(4)
    weight = ow_buf[...].reshape(C * CL, CL)

    def wait_mixed(i, carry):
        peer = lax.rem(me + N - i, N)
        mixed_copy(i, lax.rem(peer, C) * S + peer // C).wait_recv()
        return carry

    lax.fori_loop(1, N, wait_mixed, 0)
    mixed = recv_m[...].astype(jnp.float32)
    mixed = jnp.concatenate(
        [mixed[:, j * K : (j + 1) * K, :].reshape(N * K, LANES) for j in range(nb)],
        axis=1,
    ).astype(jnp.bfloat16)
    out_ref[...] = lax.dot_general(
        weight, mixed, (((0,), (0,)), ((), ())), preferred_element_type=jnp.float32
    ).astype(out_ref.dtype)

    for i in range(1, C):
        for n in range(5):
            swap(i, n, lax.rem(c + i, C), c).wait_send()

    def drain(i, carry):
        filter_copy(i, lax.rem(s + i, S), s).wait_send()
        for g in range(3):
            group_copy(g, i, lax.rem(s + i, S), s).wait_send()
        return carry

    lax.fori_loop(1, S, drain, 0)

    def drain_mixed(i, carry):
        mixed_copy(i, c * S + s).wait_send()
        return carry

    lax.fori_loop(1, N, drain_mixed, 0)


def fused(S, C, inputs, proj_weight, short_taps, skip_gain, filters, out_weight):
    CL, L = inputs.shape
    K = CL // S
    nb = L // LANES
    NB = S * nb
    N = S * C
    half, full = jnp.bfloat16, jnp.float32
    dma = pltpu.SemaphoreType.DMA
    vmem = pl.BlockSpec(memory_space=pltpu.VMEM)
    return pl.pallas_call(
        functools.partial(kernel, S, C),
        out_shape=jax.ShapeDtypeStruct((CL, L), half),
        in_specs=[vmem] * 6,
        out_specs=vmem,
        scratch_shapes=[
            pltpu.VMEM((C, CL, L), half),
            pltpu.VMEM((C, 3, CL, CL), half),
            pltpu.VMEM((C, CL, CL), half),
            pltpu.VMEM((S, nb * 2 * K, LANES), half),
            pltpu.VMEM((S, nb * 2 * K, LANES), half),
            pltpu.VMEM((3, S, nb * K, LANES), half),
            pltpu.VMEM((3, S, nb * K, LANES), half),
            pltpu.VMEM((S, nb * K, LANES), half),
            pltpu.VMEM((N, nb * K, LANES), half),
            pltpu.VMEM((NB * 2 * K, LANES), full),
            pltpu.VMEM((3, NB * K, LANES), full),
            pltpu.VMEM((NB * K, LANES), full),
            pltpu.VMEM((4, LANES // SEG, NB + NB // PARTS, LANES), full),
            pltpu.VMEM((2 * K, NB // PARTS * LANES, PARTS * SEG), half),
            pltpu.VMEM((PARTS * SEG // LANES, NB // PARTS * (LANES // SEG), LANES), full),
            pltpu.VMEM(
                (PARTS * SEG // LANES, (NB // PARTS + 2) * (LANES // SEG), LANES), full
            ),
            dma((5, C)),
            dma((5, C)),
            dma((S,)),
            dma((S,)),
            dma((3, S)),
            dma((3, S)),
            dma((N,)),
            dma((N,)),
        ],
        compiler_params=pltpu.CompilerParams(
            collective_id=0, has_side_effects=True, vmem_limit_bytes=VMEM_LIMIT
        ),
    )(
        inputs,
        proj_weight,
        short_taps.transpose(1, 2, 0),
        skip_gain.T,
        filters,
        out_weight,
    )


VMEM_LIMIT = 56 * 1024 * 1024


def fits(S, C, CL, L):
    K = CL // S
    toeplitz = 2 * K * S * L * SEG * 2
    return (
        C > 1
        and S > 1
        and CL % (8 * S) == 0
        and CL % LANES == 0
        and L % LANES == 0
        and (S * L // LANES) % (8 * PARTS) == 0
        and toeplitz <= 40 * 1024 * 1024
    )


def solution(mesh):
    in_specs = (
        P("ch", "seq"),
        P(None, "ch", None),
        P("ch", None, None),
        P("ch", None),
        P(None, "ch", "seq"),
        P("ch", None),
    )
    out_specs = P("ch", "seq")
    S, C = mesh.shape["seq"], mesh.shape["ch"]

    def body(*shards):
        if fits(S, C, *shards[0].shape):
            return fused(S, C, *shards)
        return local(*shards)

    return jax.shard_map(body, mesh=mesh, in_specs=in_specs, out_specs=out_specs, check_vma=False)
```
